32 devices in a mesh: beam: 2 (over y), chan: 8 (over z, x), tm: 2 (over core).
Axes of the slice: x: 2, y: 2, z: 4, core: 2. Of those that a mesh axis runs over, the one named last changes fastest.
Arguments:
- spectra: float32 [512, 8192], P(('beam', 'chan'), 'tm'), parts along dimension 0, may hold values from -6 to 6
- delay_shifts: int32 [8, 256], replicated, may hold values from 0 to 112, as said below
- box_widths: int32 [20], replicated, may hold values from 1 to 128, as said below
Outputs:
- pulse_power: float32 [512, 8192], P(('beam', 'chan'), 'tm'), parts along dimension 0
The draws below stay inside these ranges and needn't reach their ends.
There are 2 independent parts, one for each index of `beam`. The reference program is written for one: setup_inputs(seed, part) draws one part's arguments, and reference() takes and returns one part's arrays. A program takes and returns all parts, laid end to end along the dimension named above; an argument that names none is the same for every part. Nothing has to cross between parts.
Inputs may be any that keep to these rules, and one draw needn't show every extreme that they name: `delay_shifts`: each section's row of the table contains 112 in some column. `box_widths`: some filter has width 128.
All inputs are finite; a program needn't handle non-finite values.
Results may differ from the reference program's by a relative error of at most 0.000023.
Values sent between devices are 32-bit elements; how exact they have to be, the bound alone decides.
A program may use at most 64 MiB of HBM per device.

```python
import jax
import jax.numpy as jnp
from jax import lax

LOCAL_SECTIONS = 5
SWAP_SECTIONS = 3
SECTIONS = 8
CHANNELS = 256
TIME_DEV = 4096
TIME = 8192
SHIFT_MAX = 112
WMAX = 128
NBOX = 20
N_CHAN = 8
N_TM = 2


def draw_delay_shifts(key, part):
    drawn = jax.random.randint(jax.random.fold_in(key, 11), (SECTIONS, CHANNELS), 0, SHIFT_MAX + 1, dtype=jnp.int32)
    places = jax.random.randint(jax.random.fold_in(key, 12), (SECTIONS,), 0, CHANNELS, dtype=jnp.int32)
    chosen = jnp.arange(CHANNELS, dtype=jnp.int32)[None, :] == places[:, None]
    return jnp.where(chosen, SHIFT_MAX, drawn).astype(jnp.int32)


def draw_box_widths(key, part):
    drawn = jax.random.randint(jax.random.fold_in(key, 21), (NBOX,), 1, WMAX + 1, dtype=jnp.int32)
    places = jax.random.randint(jax.random.fold_in(key, 22), (), 0, NBOX, dtype=jnp.int32)
    chosen = jnp.arange(NBOX, dtype=jnp.int32) == places
    return jnp.where(chosen, WMAX, drawn).astype(jnp.int32)


def steps_of(key, shape, split, smallest, top_value):
    loudness, own = 1.0, jax.random.fold_in(key, 6)
    for axis_at, shards_of in split:
        draws = jnp.exp(jax.random.uniform(jax.random.fold_in(own, axis_at), (shards_of,), jnp.float32, smallest / len(split), top_value / len(split)))
        loudness = loudness * jnp.repeat(draws, shape[axis_at] // shards_of).reshape([-1 if axis == axis_at else 1 for axis in range(len(shape))])
    return loudness


def gaussian(stream_key, extent, spread, reach, split=(), held_as=jnp.bfloat16):
    values = spread * jax.random.normal(stream_key, extent, jnp.float32)
    if split:
        values = values * steps_of(stream_key, extent, split, -0.22, 0.18)
    return jnp.clip(values, -reach, reach).astype(held_as)


def setup_inputs(seed: int = 0, part: int = 0) -> dict:
    streams_of = jax.random.split(jax.random.key(seed), 4)
    own_keys = jax.random.split(jax.random.fold_in(streams_of[3], part), 4)
    return {
        "spectra": gaussian(own_keys[0], (CHANNELS, TIME), 1.0, 6.0, ((0, 8), (1, 2)), jnp.float32),
        "delay_shifts": draw_delay_shifts(jax.random.fold_in(streams_of[3], 71), part),
        "box_widths": draw_box_widths(jax.random.fold_in(streams_of[3], 71), part),
    }


root_half = 0.7071067811865476


def pair_rows(series, stride):
    total_rows, length = series.shape
    paired = series.reshape(total_rows // (2 * stride), 2, stride, length)
    lower = jnp.broadcast_to(paired[:, 0:1], paired.shape).reshape(total_rows, length)
    upper = jnp.broadcast_to(paired[:, 1:2], paired.shape).reshape(total_rows, length)
    return lower, upper


def delay_add(lower, upper_wide, shifts):
    length = lower.shape[1]

    def take_single(single, shift_by):
        return lax.dynamic_slice_in_dim(single, SHIFT_MAX - shift_by, length)

    delayed = jax.vmap(take_single)(upper_wide, shifts)
    return (lower + delayed) * root_half


def section(series, stride, shifts):
    lower, upper = pair_rows(series, stride)
    upper_wide = jnp.pad(upper, ((0, 0), (SHIFT_MAX, 0)))
    return delay_add(lower, upper_wide, shifts)


def boxcar_power(segment, box_widths):
    length = segment.shape[1] - WMAX
    running = jnp.cumsum(segment, axis=1)
    closing = running[:, WMAX:]

    def add_filter(which, summed):
        span_width = box_widths[which]
        opening = lax.dynamic_slice_in_dim(running, WMAX - span_width, length, 1)
        window_sum = closing - opening
        return summed + window_sum * window_sum / span_width.astype(jnp.float32)

    summed = lax.fori_loop(0, NBOX, add_filter, jnp.zeros(closing.shape, jnp.float32))
    return summed / NBOX


def reference(spectra, delay_shifts, box_widths):
    series = spectra
    for level in range(LOCAL_SECTIONS):
        series = section(series, 2 ** level, delay_shifts[level])
    chan_bits = N_CHAN.bit_length() - 1
    for swap_step in range(SWAP_SECTIONS):
        stride = 2 ** (LOCAL_SECTIONS + chan_bits - SWAP_SECTIONS + swap_step)
        series = section(series, stride, delay_shifts[LOCAL_SECTIONS + swap_step])
    padded = jnp.pad(series, ((0, 0), (WMAX, 0)))
    pieces = []
    for block in range(N_TM):
        segment = padded[:, block * TIME_DEV: block * TIME_DEV + WMAX + TIME_DEV]
        pieces.append(boxcar_power(segment, box_widths))
    return jnp.concatenate(pieces, axis=1)
```

```python
import functools

import jax
import jax.numpy as jnp
from jax import lax
from jax.experimental import pallas as pl
from jax.experimental.pallas import tpu as pltpu
from jax.sharding import PartitionSpec as P

SWAPS = 3
LANES = 128
SUB = 8
CHUNKS = 8
MESH = pl.DeviceIdType.MESH


def kernel(shifts_ref, widths_ref, x_ref, out_ref, raw, y, recv, prev, amounts, done, edge, sums,
           load_sem, tail_send, tail_recv, send_sem, recv_sem, hist_send, hist_recv, out_sem):
    rows, time_len = x_ref.shape
    groups = rows // SUB
    levels = rows.bit_length() - 1
    sections = shifts_ref.shape[0]
    boxes = widths_ref.shape[0]
    hist = sections
    tiles = time_len // LANES
    per = tiles // CHUNKS
    chan, tm = lax.axis_index("chan"), lax.axis_index("tm")
    chans, tms = lax.axis_size("chan"), lax.axis_size("tm")
    chan_bits = chans.bit_length() - 1
    bits = [(chan // 2 ** (chan_bits - SWAPS + s)) % 2 for s in range(SWAPS)]
    peers = [chan + (1 - 2 * bits[s]) * 2 ** (chan_bits - SWAPS + s) for s in range(SWAPS)]

    def cols(first, count=1):
        return pl.ds(pl.multiple_of(first * LANES, LANES), count * LANES)

    load = pltpu.make_async_copy(x_ref, raw.at[:, pl.ds(hist * LANES, time_len)], load_sem)
    load.start()

    barrier = pltpu.get_barrier_semaphore()
    for s in range(SWAPS):
        pl.semaphore_signal(barrier, inc=1, device_id={"chan": peers[s]}, device_id_type=MESH)

    @pl.when(tm > 0)
    def _():
        pl.semaphore_signal(barrier, inc=1, device_id={"tm": tm - 1}, device_id_type=MESH)

    sub = lax.broadcasted_iota(jnp.int32, (SUB, LANES), 0)
    lane = lax.broadcasted_iota(jnp.int32, (SUB, LANES), 1)

    def fill(j, _):
        for g in range(groups):
            v = jnp.zeros((SUB, LANES), jnp.int32)
            for r in range(SUB):
                v = jnp.where(sub == r, shifts_ref[j, chan * rows + g * SUB + r], v)
            amounts[j, g * SUB:(g + 1) * SUB, :] = v
        return 0

    lax.fori_loop(0, sections, fill, 0)
    prev[...] = jnp.zeros_like(prev)

    pl.semaphore_wait(barrier, SWAPS + jnp.where(tm < tms - 1, 1, 0))

    def tail():
        return pltpu.make_async_remote_copy(
            src_ref=x_ref.at[:, pl.ds(time_len - hist * LANES, hist * LANES)],
            dst_ref=raw.at[:, pl.ds(0, hist * LANES)],
            send_sem=tail_send, recv_sem=tail_recv,
            device_id={"tm": (tm + 1) % tms}, device_id_type=MESH)

    @pl.when(tm < tms - 1)
    def _():
        tail().start()

    def swap(s, c):
        where = cols(hist + c * per, per)
        return pltpu.make_async_remote_copy(
            src_ref=y.at[s, :, where], dst_ref=recv.at[s, :, where],
            send_sem=send_sem.at[s, c], recv_sem=recv_sem.at[s, c],
            device_id={"chan": peers[s]}, device_id_type=MESH)

    def swap_hist(s):
        first = levels - 1 + s
        where = cols(first, hist - first)
        return pltpu.make_async_remote_copy(
            src_ref=y.at[s, :, where], dst_ref=recv.at[s, :, where],
            send_sem=hist_send.at[s], recv_sem=hist_recv.at[s],
            device_id={"chan": peers[s]}, device_id_type=MESH)

    def delayed(j, g, now, before):
        amount = amounts[j, g * SUB:(g + 1) * SUB, :]
        mixed = jnp.where(lane < LANES - amount, now, before)
        return jnp.take_along_axis(mixed, (lane - amount) & (LANES - 1), axis=1, mode="promise_in_bounds")

    def own_sections(first, count):
        kept = [[prev[j, g * SUB:(g + 1) * SUB, :] for g in range(groups)] for j in range(levels)]
        for t in range(count):
            k = first + t
            v = [raw[g * SUB:(g + 1) * SUB, cols(k)] for g in range(groups)]
            for j in range(levels):
                stride = 2 ** j
                if stride < SUB:
                    high = (sub & stride) != 0
                    low = [jnp.where(high, pltpu.roll(a, stride, 0), a) for a in v]
                    up = [jnp.where(high, a, pltpu.roll(a, SUB - stride, 0)) for a in v]
                else:
                    step = stride // SUB
                    low = [v[g & ~step] for g in range(groups)]
                    up = [v[g | step] for g in range(groups)]
                v = [low[g] + delayed(j, g, up[g], kept[j][g]) for g in range(groups)]
                kept[j] = up
            for g in range(groups):
                y[0, g * SUB:(g + 1) * SUB, cols(k)] = v[g]
        for j in range(levels):
            for g in range(groups):
                prev[j, g * SUB:(g + 1) * SUB, :] = kept[j][g]

    def swap_section(s, first, count, put):
        is_low = bits[s] == 0
        for g in range(groups):
            rs = slice(g * SUB, (g + 1) * SUB)
            before = jnp.where(is_low, recv[s, rs, cols(first - 1)], y[s, rs, cols(first - 1)])
            for t in range(count):
                own, other = y[s, rs, cols(first + t)], recv[s, rs, cols(first + t)]
                up = jnp.where(is_low, other, own)
                low = jnp.where(is_low, own, other)
                put(g, t, low + delayed(levels + s, g, up, before))
                before = up

    def put_next(s, first):
        def put(g, t, value):
            y[s + 1, g * SUB:(g + 1) * SUB, cols(first + t)] = value
        return put

    def put_done(g, t, value):
        done[t * rows + g * SUB:t * rows + (g + 1) * SUB, :] = value

    a = lax.broadcasted_iota(jnp.int32, (LANES, 2 * LANES), 0)
    b = lax.broadcasted_iota(jnp.int32, (LANES, 2 * LANES), 1)
    ones = jnp.where(b < LANES, jnp.where(a <= b, 1.0, 0.0), jnp.where(a > b - LANES, -1.0, 0.0)).astype(jnp.bfloat16)

    def prefixes(x):
        total = None
        for _ in range(3):
            piece = x.astype(jnp.bfloat16)
            part = jnp.dot(piece, ones, preferred_element_type=jnp.float32)
            total = part if total is None else total + part
            x = x - piece.astype(jnp.float32)
        return total

    edge[...] = jnp.zeros_like(edge)

    @pl.when(tm == 0)
    def _():
        for s in range(SWAPS):
            y[s, :, cols(hist - 1)] = jnp.zeros((rows, LANES), jnp.float32)
            recv[s, :, cols(hist - 1)] = jnp.zeros((rows, LANES), jnp.float32)

    load.wait()

    @pl.when(tm > 0)
    def _():
        tail().wait_recv()
        own_sections(0, hist)
        swap_hist(0).start()

    def first_loop(c, _):
        own_sections(hist + c * per, per)
        swap(0, c).start()
        return 0

    lax.fori_loop(0, CHUNKS, first_loop, 0)

    box_lane = lax.broadcasted_iota(jnp.int32, (rows, LANES), 1)
    scale = 0.5 ** sections / boxes

    def out_copy(c):
        where = cols(c * per, per)
        return pltpu.make_async_copy(raw.at[:, where], out_ref.at[:, where], out_sem.at[c])

    def boxcars(c):
        sums[...] = prefixes(done[...])
        for t in range(per):
            now = sums[t * rows:(t + 1) * rows, :LANES]
            before = edge[...] if t == 0 else sums[(t - 1) * rows:t * rows, LANES:]
            power = jnp.zeros((rows, LANES), jnp.float32)
            for f in range(boxes):
                width = widths_ref[f]
                mixed = jnp.where(box_lane < LANES - width, now, before)
                window = now - pltpu.roll(mixed, width & (LANES - 1), 1)
                power = power + window * window * (scale / jnp.full((rows, LANES), width, jnp.int32).astype(jnp.float32))
            raw[:, cols(c * per + t)] = power
        edge[...] = sums[(per - 1) * rows:, LANES:]

    def step(i, _):
        @pl.when(i < CHUNKS)
        def _():
            @pl.when((i == 0) & (tm > 0))
            def _():
                swap_hist(0).wait_recv()
                swap_section(0, levels, hist - levels, put_next(0, levels))
                swap_hist(1).start()
            swap(0, i).wait_recv()
            first = hist + i * per
            swap_section(0, first, per, put_next(0, first))
            swap(1, i).start()

        @pl.when((i >= 1) & (i <= CHUNKS))
        def _():
            c = i - 1
            @pl.when((c == 0) & (tm > 0))
            def _():
                swap_hist(1).wait_recv()
                swap_section(1, levels + 1, hist - levels - 1, put_next(1, levels + 1))
                swap_hist(2).start()
            swap(1, c).wait_recv()
            first = hist + c * per
            swap_section(1, first, per, put_next(1, first))
            swap(2, c).start()

        @pl.when(i >= 2)
        def _():
            c = i - 2
            @pl.when((c == 0) & (tm > 0))
            def _():
                swap_hist(2).wait_recv()
                swap_section(2, hist - 1, 1, put_done)
                edge[...] = prefixes(done[0:rows, :])[:, LANES:]
            swap(2, c).wait_recv()
            swap_section(2, hist + c * per, per, put_done)
            boxcars(c)
            out_copy(c).start()

        return 0

    lax.fori_loop(0, CHUNKS + 2, step, 0)

    def finish(c, _):
        for s in range(SWAPS):
            swap(s, c).wait_send()
        out_copy(c).wait()
        return 0

    lax.fori_loop(0, CHUNKS, finish, 0)

    @pl.when(tm > 0)
    def _():
        for s in range(SWAPS):
            swap_hist(s).wait_send()

    @pl.when(tm < tms - 1)
    def _():
        tail().wait_send()


def local(spectra, delay_shifts, box_widths):
    rows, time_len = spectra.shape
    sections = delay_shifts.shape[0]
    levels = rows.bit_length() - 1
    width = time_len + sections * LANES
    per = time_len // LANES // CHUNKS
    dma = pltpu.SemaphoreType.DMA
    return pl.pallas_call(
        kernel,
        out_shape=jax.ShapeDtypeStruct((rows, time_len), jnp.float32),
        in_specs=[pl.BlockSpec(memory_space=pltpu.SMEM), pl.BlockSpec(memory_space=pltpu.SMEM),
                  pl.BlockSpec(memory_space=pl.ANY)],
        out_specs=pl.BlockSpec(memory_space=pl.ANY),
        scratch_shapes=[
            pltpu.VMEM((rows, width), jnp.float32),
            pltpu.VMEM((SWAPS, rows, width), jnp.float32),
            pltpu.VMEM((SWAPS, rows, width), jnp.float32),
            pltpu.VMEM((levels, rows, LANES), jnp.float32),
            pltpu.VMEM((sections, rows, LANES), jnp.int32),
            pltpu.VMEM((per * rows, LANES), jnp.float32),
            pltpu.VMEM((rows, LANES), jnp.float32),
            pltpu.VMEM((per * rows, 2 * LANES), jnp.float32),
            dma(()), dma(()), dma(()),
            dma((SWAPS, CHUNKS)), dma((SWAPS, CHUNKS)),
            dma((SWAPS,)), dma((SWAPS,)), dma((CHUNKS,)),
        ],
        compiler_params=pltpu.CompilerParams(
            collective_id=0, has_side_effects=True, vmem_limit_bytes=32 * 1024 * 1024),
    )(delay_shifts, box_widths, spectra)


def solution(mesh):
    in_specs = (P(("beam", "chan"), "tm"), P(), P())
    out_specs = P(("beam", "chan"), "tm")
    return jax.shard_map(local, mesh=mesh, in_specs=in_specs, out_specs=out_specs, check_vma=False)
```

```python
import functools

import jax
import jax.numpy as jnp
from jax import lax
from jax.experimental import pallas as pl
from jax.experimental.pallas import tpu as pltpu
from jax.sharding import PartitionSpec as P

SWAPS = 3
LANES = 128
SUB = 8
CHUNKS = 8
MESH = pl.DeviceIdType.MESH


def kernel(shifts_ref, widths_ref, x_ref, out_ref, raw, y, recv, prev, amounts, done, edge, sums,
           load_sem, tail_send, tail_recv, send_sem, recv_sem, hist_send, hist_recv, out_sem):
    rows, time_len = x_ref.shape
    groups = rows // SUB
    levels = rows.bit_length() - 1
    sections = shifts_ref.shape[0]
    boxes = widths_ref.shape[0]
    hist = sections
    tiles = time_len // LANES
    per = tiles // CHUNKS
    chan, tm = lax.axis_index("chan"), lax.axis_index("tm")
    chans, tms = lax.axis_size("chan"), lax.axis_size("tm")
    chan_bits = chans.bit_length() - 1
    bits = [(chan // 2 ** (chan_bits - SWAPS + s)) % 2 for s in range(SWAPS)]
    peers = [chan + (1 - 2 * bits[s]) * 2 ** (chan_bits - SWAPS + s) for s in range(SWAPS)]

    def cols(first, count=1):
        return pl.ds(pl.multiple_of(first * LANES, LANES), count * LANES)

    load = pltpu.make_async_copy(x_ref, raw.at[:, pl.ds(hist * LANES, time_len)], load_sem)
    load.start()

    barrier = pltpu.get_barrier_semaphore()
    for s in range(SWAPS):
        pl.semaphore_signal(barrier, inc=1, device_id={"chan": peers[s]}, device_id_type=MESH)

    @pl.when(tm > 0)
    def _():
        pl.semaphore_signal(barrier, inc=1, device_id={"tm": tm - 1}, device_id_type=MESH)

    sub = lax.broadcasted_iota(jnp.int32, (SUB, LANES), 0)
    lane = lax.broadcasted_iota(jnp.int32, (SUB, LANES), 1)

    def fill(j, _):
        for g in range(groups):
            v = jnp.zeros((SUB, LANES), jnp.int32)
            for r in range(SUB):
                v = jnp.where(sub == r, shifts_ref[j, chan * rows + g * SUB + r], v)
            amounts[j, g * SUB:(g + 1) * SUB, :] = v
        return 0

    lax.fori_loop(0, sections, fill, 0)
    prev[...] = jnp.zeros_like(prev)

    pl.semaphore_wait(barrier, SWAPS + jnp.where(tm < tms - 1, 1, 0))

    def tail():
        return pltpu.make_async_remote_copy(
            src_ref=x_ref.at[:, pl.ds(time_len - hist * LANES, hist * LANES)],
            dst_ref=raw.at[:, pl.ds(0, hist * LANES)],
            send_sem=tail_send, recv_sem=tail_recv,
            device_id={"tm": (tm + 1) % tms}, device_id_type=MESH)

    @pl.when(tm < tms - 1)
    def _():
        tail().start()

    def swap(s, c):
        where = cols(hist + c * per, per)
        return pltpu.make_async_remote_copy(
            src_ref=y.at[s, :, where], dst_ref=recv.at[s, :, where],
            send_sem=send_sem.at[s, c], recv_sem=recv_sem.at[s, c],
            device_id={"chan": peers[s]}, device_id_type=MESH)

    def swap_hist(s):
        first = levels - 1 + s
        where = cols(first, hist - first)
        return pltpu.make_async_remote_copy(
            src_ref=y.at[s, :, where], dst_ref=recv.at[s, :, where],
            send_sem=hist_send.at[s], recv_sem=hist_recv.at[s],
            device_id={"chan": peers[s]}, device_id_type=MESH)

    def delayed(j, g, now, before):
        amount = amounts[j, g * SUB:(g + 1) * SUB, :]
        mixed = jnp.where(lane < LANES - amount, now, before)
        return jnp.take_along_axis(mixed, (lane - amount) & (LANES - 1), axis=1, mode="promise_in_bounds")

    def own_sections(first, count):
        kept = [[prev[j, g * SUB:(g + 1) * SUB, :] for g in range(groups)] for j in range(levels)]
        for t in range(count):
            k = first + t
            v = [raw[g * SUB:(g + 1) * SUB, cols(k)] for g in range(groups)]
            for j in range(levels):
                stride = 2 ** j
                if stride < SUB:
                    high = (sub & stride) != 0
                    low = [jnp.where(high, pltpu.roll(a, stride, 0), a) for a in v]
                    up = [jnp.where(high, a, pltpu.roll(a, SUB - stride, 0)) for a in v]
                else:
                    step = stride // SUB
                    low = [v[g & ~step] for g in range(groups)]
                    up = [v[g | step] for g in range(groups)]
                v = [low[g] + delayed(j, g, up[g], kept[j][g]) for g in range(groups)]
                kept[j] = up
            for g in range(groups):
                y[0, g * SUB:(g + 1) * SUB, cols(k)] = v[g]
        for j in range(levels):
            for g in range(groups):
                prev[j, g * SUB:(g + 1) * SUB, :] = kept[j][g]

    def swap_section(s, first, count, put):
        is_low = bits[s] == 0
        held = []
        for g in range(groups):
            rs = slice(g * SUB, (g + 1) * SUB)
            before = jnp.where(is_low, recv[s, rs, cols(first - 1)], y[s, rs, cols(first - 1)])
            own = [y[s, rs, cols(first + t)] for t in range(count)]
            other = [recv[s, rs, cols(first + t)] for t in range(count)]
            low = [jnp.where(is_low, a, b) for a, b in zip(own, other)]
            up = [jnp.where(is_low, b, a) for a, b in zip(own, other)]
            held.append((low, [before] + up))
        values = [[low[t] + delayed(levels + s, g, up[t + 1], up[t]) for t in range(count)]
                  for g, (low, up) in enumerate(held)]
        for g in range(groups):
            for t in range(count):
                put(g, t, values[g][t])

    def put_next(s, first):
        def put(g, t, value):
            y[s + 1, g * SUB:(g + 1) * SUB, cols(first + t)] = value
        return put

    def put_done(g, t, value):
        done[t * rows + g * SUB:t * rows + (g + 1) * SUB, :] = value

    a = lax.broadcasted_iota(jnp.int32, (LANES, 2 * LANES), 0)
    b = lax.broadcasted_iota(jnp.int32, (LANES, 2 * LANES), 1)
    ones = jnp.where(b < LANES, jnp.where(a <= b, 1.0, 0.0), jnp.where(a > b - LANES, -1.0, 0.0)).astype(jnp.bfloat16)

    def prefixes(x):
        total = None
        for _ in range(3):
            piece = x.astype(jnp.bfloat16)
            part = jnp.dot(piece, ones, preferred_element_type=jnp.float32)
            total = part if total is None else total + part
            x = x - piece.astype(jnp.float32)
        return total

    edge[...] = jnp.zeros_like(edge)

    @pl.when(tm == 0)
    def _():
        for s in range(SWAPS):
            y[s, :, cols(hist - 1)] = jnp.zeros((rows, LANES), jnp.float32)
            recv[s, :, cols(hist - 1)] = jnp.zeros((rows, LANES), jnp.float32)

    load.wait()

    @pl.when(tm > 0)
    def _():
        tail().wait_recv()
        own_sections(0, hist)
        swap_hist(0).start()

    def first_loop(c, _):
        own_sections(hist + c * per, per)
        swap(0, c).start()
        return 0

    lax.fori_loop(0, CHUNKS, first_loop, 0)

    box_lane = lax.broadcasted_iota(jnp.int32, (rows, LANES), 1)
    scale = 0.5 ** sections / boxes

    def out_copy(c):
        where = cols(c * per, per)
        return pltpu.make_async_copy(raw.at[:, where], out_ref.at[:, where], out_sem.at[c])

    def boxcars(c):
        sums[...] = prefixes(done[...])
        for t in range(per):
            now = sums[t * rows:(t + 1) * rows, :LANES]
            before = edge[...] if t == 0 else sums[(t - 1) * rows:t * rows, LANES:]
            power = jnp.zeros((rows, LANES), jnp.float32)
            for f in range(boxes):
                width = widths_ref[f]
                mixed = jnp.where(box_lane < LANES - width, now, before)
                window = now - pltpu.roll(mixed, width & (LANES - 1), 1)
                power = power + window * window * (scale / jnp.full((rows, LANES), width, jnp.int32).astype(jnp.float32))
            raw[:, cols(c * per + t)] = power
        edge[...] = sums[(per - 1) * rows:, LANES:]

    def step(i, _):
        @pl.when(i < CHUNKS)
        def _():
            @pl.when((i == 0) & (tm > 0))
            def _():
                swap_hist(0).wait_recv()
                swap_section(0, levels, hist - levels, put_next(0, levels))
                swap_hist(1).start()
            swap(0, i).wait_recv()
            first = hist + i * per
            swap_section(0, first, per, put_next(0, first))
            swap(1, i).start()

        @pl.when((i >= 1) & (i <= CHUNKS))
        def _():
            c = i - 1
            @pl.when((c == 0) & (tm > 0))
            def _():
                swap_hist(1).wait_recv()
                swap_section(1, levels + 1, hist - levels - 1, put_next(1, levels + 1))
                swap_hist(2).start()
            swap(1, c).wait_recv()
            first = hist + c * per
            swap_section(1, first, per, put_next(1, first))
            swap(2, c).start()

        @pl.when(i >= 2)
        def _():
            c = i - 2
            @pl.when((c == 0) & (tm > 0))
            def _():
                swap_hist(2).wait_recv()
                swap_section(2, hist - 1, 1, put_done)
                edge[...] = prefixes(done[0:rows, :])[:, LANES:]
            swap(2, c).wait_recv()
            swap_section(2, hist + c * per, per, put_done)
            boxcars(c)
            out_copy(c).start()

        return 0

    lax.fori_loop(0, CHUNKS + 2, step, 0)

    def finish(c, _):
        for s in range(SWAPS):
            swap(s, c).wait_send()
        out_copy(c).wait()
        return 0

    lax.fori_loop(0, CHUNKS, finish, 0)

    @pl.when(tm > 0)
    def _():
        for s in range(SWAPS):
            swap_hist(s).wait_send()

    @pl.when(tm < tms - 1)
    def _():
        tail().wait_send()


def local(spectra, delay_shifts, box_widths):
    rows, time_len = spectra.shape
    sections = delay_shifts.shape[0]
    levels = rows.bit_length() - 1
    width = time_len + sections * LANES
    per = time_len // LANES // CHUNKS
    dma = pltpu.SemaphoreType.DMA
    return pl.pallas_call(
        kernel,
        out_shape=jax.ShapeDtypeStruct((rows, time_len), jnp.float32),
        in_specs=[pl.BlockSpec(memory_space=pltpu.SMEM), pl.BlockSpec(memory_space=pltpu.SMEM),
                  pl.BlockSpec(memory_space=pl.ANY)],
        out_specs=pl.BlockSpec(memory_space=pl.ANY),
        scratch_shapes=[
            pltpu.VMEM((rows, width), jnp.float32),
            pltpu.VMEM((SWAPS, rows, width), jnp.float32),
            pltpu.VMEM((SWAPS, rows, width), jnp.float32),
            pltpu.VMEM((levels, rows, LANES), jnp.float32),
            pltpu.VMEM((sections, rows, LANES), jnp.int32),
            pltpu.VMEM((per * rows, LANES), jnp.float32),
            pltpu.VMEM((rows, LANES), jnp.float32),
            pltpu.VMEM((per * rows, 2 * LANES), jnp.float32),
            dma(()), dma(()), dma(()),
            dma((SWAPS, CHUNKS)), dma((SWAPS, CHUNKS)),
            dma((SWAPS,)), dma((SWAPS,)), dma((CHUNKS,)),
        ],
        compiler_params=pltpu.CompilerParams(
            collective_id=0, has_side_effects=True, vmem_limit_bytes=32 * 1024 * 1024),
    )(delay_shifts, box_widths, spectra)


def solution(mesh):
    in_specs = (P(("beam", "chan"), "tm"), P(), P())
    out_specs = P(("beam", "chan"), "tm")
    return jax.shard_map(local, mesh=mesh, in_specs=in_specs, out_specs=out_specs, check_vma=False)
```

```python
import functools

import jax
import jax.numpy as jnp
from jax import lax
from jax.experimental import pallas as pl
from jax.experimental.pallas import tpu as pltpu
from jax.sharding import PartitionSpec as P

SWAPS = 3
LANES = 128
SUB = 8
CHUNKS = 8
LAGS = (1, 2, 4)
MESH = pl.DeviceIdType.MESH


def kernel(shifts_ref, widths_ref, x_ref, out_ref, raw, y, recv, prev, amounts, done, edge, sums,
           load_sem, tail_send, tail_recv, send_sem, recv_sem, hist_send, hist_recv, out_sem):
    rows, time_len = x_ref.shape
    groups = rows // SUB
    levels = rows.bit_length() - 1
    sections = shifts_ref.shape[0]
    boxes = widths_ref.shape[0]
    hist = sections
    tiles = time_len // LANES
    per = tiles // CHUNKS
    chan, tm = lax.axis_index("chan"), lax.axis_index("tm")
    chans, tms = lax.axis_size("chan"), lax.axis_size("tm")
    chan_bits = chans.bit_length() - 1
    bits = [(chan // 2 ** (chan_bits - SWAPS + s)) % 2 for s in range(SWAPS)]
    peers = [chan + (1 - 2 * bits[s]) * 2 ** (chan_bits - SWAPS + s) for s in range(SWAPS)]

    def cols(first, count=1):
        return pl.ds(pl.multiple_of(first * LANES, LANES), count * LANES)

    load = pltpu.make_async_copy(x_ref, raw.at[:, pl.ds(hist * LANES, time_len)], load_sem)
    load.start()

    barrier = pltpu.get_barrier_semaphore()
    for s in range(SWAPS):
        pl.semaphore_signal(barrier, inc=1, device_id={"chan": peers[s]}, device_id_type=MESH)

    @pl.when(tm > 0)
    def _():
        pl.semaphore_signal(barrier, inc=1, device_id={"tm": tm - 1}, device_id_type=MESH)

    sub = lax.broadcasted_iota(jnp.int32, (SUB, LANES), 0)
    lane = lax.broadcasted_iota(jnp.int32, (SUB, LANES), 1)

    def fill(j, _):
        for g in range(groups):
            v = jnp.zeros((SUB, LANES), jnp.int32)
            for r in range(SUB):
                v = jnp.where(sub == r, shifts_ref[j, chan * rows + g * SUB + r], v)
            amounts[j, g * SUB:(g + 1) * SUB, :] = v
        return 0

    lax.fori_loop(0, sections, fill, 0)
    prev[...] = jnp.zeros_like(prev)

    pl.semaphore_wait(barrier, SWAPS + jnp.where(tm < tms - 1, 1, 0))

    def tail():
        return pltpu.make_async_remote_copy(
            src_ref=x_ref.at[:, pl.ds(time_len - hist * LANES, hist * LANES)],
            dst_ref=raw.at[:, pl.ds(0, hist * LANES)],
            send_sem=tail_send, recv_sem=tail_recv,
            device_id={"tm": (tm + 1) % tms}, device_id_type=MESH)

    @pl.when(tm < tms - 1)
    def _():
        tail().start()

    def swap(s, c):
        where = pl.ds(hist + c * per, per)
        return pltpu.make_async_remote_copy(
            src_ref=y.at[s, where], dst_ref=recv.at[s, where],
            send_sem=send_sem.at[s, c], recv_sem=recv_sem.at[s, c],
            device_id={"chan": peers[s]}, device_id_type=MESH)

    def swap_hist(s):
        first = levels - 1 + s
        where = pl.ds(first, hist - first)
        return pltpu.make_async_remote_copy(
            src_ref=y.at[s, where], dst_ref=recv.at[s, where],
            send_sem=hist_send.at[s], recv_sem=hist_recv.at[s],
            device_id={"chan": peers[s]}, device_id_type=MESH)

    def delayed(j, g, now, before):
        amount = amounts[j, g * SUB:(g + 1) * SUB, :]
        mixed = jnp.where(lane < LANES - amount, now, before)
        return jnp.take_along_axis(mixed, (lane - amount) & (LANES - 1), axis=1, mode="promise_in_bounds")

    def own_sections(first, count):
        kept = [[prev[j, g * SUB:(g + 1) * SUB, :] for g in range(groups)] for j in range(levels)]
        for t in range(count):
            k = first + t
            v = [raw[g * SUB:(g + 1) * SUB, cols(k)] for g in range(groups)]
            for j in range(levels):
                stride = 2 ** j
                if stride < SUB:
                    high = (sub & stride) != 0
                    low = [jnp.where(high, pltpu.roll(a, stride, 0), a) for a in v]
                    up = [jnp.where(high, a, pltpu.roll(a, SUB - stride, 0)) for a in v]
                else:
                    step = stride // SUB
                    low = [v[g & ~step] for g in range(groups)]
                    up = [v[g | step] for g in range(groups)]
                v = [low[g] + delayed(j, g, up[g], kept[j][g]) for g in range(groups)]
                kept[j] = up
            for g in range(groups):
                y[0, k, g * SUB:(g + 1) * SUB, :] = v[g]
        for j in range(levels):
            for g in range(groups):
                prev[j, g * SUB:(g + 1) * SUB, :] = kept[j][g]

    def swap_section(s, first, count, put):
        is_low = bits[s] == 0
        held = []
        for g in range(groups):
            rs = slice(g * SUB, (g + 1) * SUB)
            before = jnp.where(is_low, recv[s, first - 1, rs, :], y[s, first - 1, rs, :])
            own = [y[s, first + t, rs, :] for t in range(count)]
            other = [recv[s, first + t, rs, :] for t in range(count)]
            low = [jnp.where(is_low, a, b) for a, b in zip(own, other)]
            up = [jnp.where(is_low, b, a) for a, b in zip(own, other)]
            held.append((low, [before] + up))
        values = [[low[t] + delayed(levels + s, g, up[t + 1], up[t]) for t in range(count)]
                  for g, (low, up) in enumerate(held)]
        for g in range(groups):
            for t in range(count):
                put(g, t, values[g][t])

    def put_next(s, first):
        def put(g, t, value):
            y[s + 1, first + t, g * SUB:(g + 1) * SUB, :] = value
        return put

    def put_done(g, t, value):
        done[t * rows + g * SUB:t * rows + (g + 1) * SUB, :] = value

    a = lax.broadcasted_iota(jnp.int32, (LANES, 2 * LANES), 0)
    b = lax.broadcasted_iota(jnp.int32, (LANES, 2 * LANES), 1)
    ones = jnp.where(b < LANES, jnp.where(a <= b, 1.0, 0.0), jnp.where(a > b - LANES, -1.0, 0.0)).astype(jnp.bfloat16)

    def prefixes(x):
        total = None
        for _ in range(3):
            piece = x.astype(jnp.bfloat16)
            part = jnp.dot(piece, ones, preferred_element_type=jnp.float32)
            total = part if total is None else total + part
            x = x - piece.astype(jnp.float32)
        return total

    edge[...] = jnp.zeros_like(edge)

    @pl.when(tm == 0)
    def _():
        for s in range(SWAPS):
            y[s, hist - 1] = jnp.zeros((rows, LANES), jnp.float32)
            recv[s, hist - 1] = jnp.zeros((rows, LANES), jnp.float32)

    load.wait()

    @pl.when(tm > 0)
    def _():
        tail().wait_recv()
        own_sections(0, hist)
        swap_hist(0).start()

    box_lane = lax.broadcasted_iota(jnp.int32, (rows, LANES), 1)
    scale = 0.5 ** sections / boxes

    def out_copy(c):
        where = cols(c * per, per)
        return pltpu.make_async_copy(raw.at[:, where], out_ref.at[:, where], out_sem.at[c])

    def boxcars(c):
        sums[...] = prefixes(done[...])
        for t in range(per):
            now = sums[t * rows:(t + 1) * rows, :LANES]
            before = edge[...] if t == 0 else sums[(t - 1) * rows:t * rows, LANES:]
            power = jnp.zeros((rows, LANES), jnp.float32)
            for f in range(boxes):
                width = widths_ref[f]
                mixed = jnp.where(box_lane < LANES - width, now, before)
                window = now - pltpu.roll(mixed, width & (LANES - 1), 1)
                power = power + window * window * (scale / jnp.full((rows, LANES), width, jnp.int32).astype(jnp.float32))
            raw[:, cols(c * per + t)] = power
        edge[...] = sums[(per - 1) * rows:, LANES:]

    def step(i, _):
        @pl.when(i < CHUNKS)
        def _():
            own_sections(hist + i * per, per)
            swap(0, i).start()

        @pl.when((i >= LAGS[0]) & (i < CHUNKS + LAGS[0]))
        def _():
            c = i - LAGS[0]
            @pl.when((c == 0) & (tm > 0))
            def _():
                swap_hist(0).wait_recv()
                swap_section(0, levels, hist - levels, put_next(0, levels))
                swap_hist(1).start()
            swap(0, c).wait_recv()
            first = hist + c * per
            swap_section(0, first, per, put_next(0, first))
            swap(1, c).start()

        @pl.when((i >= LAGS[1]) & (i < CHUNKS + LAGS[1]))
        def _():
            c = i - LAGS[1]
            @pl.when((c == 0) & (tm > 0))
            def _():
                swap_hist(1).wait_recv()
                swap_section(1, levels + 1, hist - levels - 1, put_next(1, levels + 1))
                swap_hist(2).start()
            swap(1, c).wait_recv()
            first = hist + c * per
            swap_section(1, first, per, put_next(1, first))
            swap(2, c).start()

        @pl.when(i >= LAGS[2])
        def _():
            c = i - LAGS[2]
            @pl.when((c == 0) & (tm > 0))
            def _():
                swap_hist(2).wait_recv()
                swap_section(2, hist - 1, 1, put_done)
                edge[...] = prefixes(done[0:rows, :])[:, LANES:]
            swap(2, c).wait_recv()
            swap_section(2, hist + c * per, per, put_done)
            boxcars(c)
            out_copy(c).start()

        return 0

    lax.fori_loop(0, CHUNKS + LAGS[2], step, 0)

    def finish(c, _):
        for s in range(SWAPS):
            swap(s, c).wait_send()
        out_copy(c).wait()
        return 0

    lax.fori_loop(0, CHUNKS, finish, 0)

    @pl.when(tm > 0)
    def _():
        for s in range(SWAPS):
            swap_hist(s).wait_send()

    @pl.when(tm < tms - 1)
    def _():
        tail().wait_send()


def local(spectra, delay_shifts, box_widths):
    rows, time_len = spectra.shape
    sections = delay_shifts.shape[0]
    levels = rows.bit_length() - 1
    width = time_len + sections * LANES
    per = time_len // LANES // CHUNKS
    dma = pltpu.SemaphoreType.DMA
    return pl.pallas_call(
        kernel,
        out_shape=jax.ShapeDtypeStruct((rows, time_len), jnp.float32),
        in_specs=[pl.BlockSpec(memory_space=pltpu.SMEM), pl.BlockSpec(memory_space=pltpu.SMEM),
                  pl.BlockSpec(memory_space=pl.ANY)],
        out_specs=pl.BlockSpec(memory_space=pl.ANY),
        scratch_shapes=[
            pltpu.VMEM((rows, width), jnp.float32),
            pltpu.VMEM((SWAPS, width // LANES, rows, LANES), jnp.float32),
            pltpu.VMEM((SWAPS, width // LANES, rows, LANES), jnp.float32),
            pltpu.VMEM((levels, rows, LANES), jnp.float32),
            pltpu.VMEM((sections, rows, LANES), jnp.int32),
            pltpu.VMEM((per * rows, LANES), jnp.float32),
            pltpu.VMEM((rows, LANES), jnp.float32),
            pltpu.VMEM((per * rows, 2 * LANES), jnp.float32),
            dma(()), dma(()), dma(()),
            dma((SWAPS, CHUNKS)), dma((SWAPS, CHUNKS)),
            dma((SWAPS,)), dma((SWAPS,)), dma((CHUNKS,)),
        ],
        compiler_params=pltpu.CompilerParams(
            collective_id=0, has_side_effects=True, vmem_limit_bytes=60 * 1024 * 1024),
    )(delay_shifts, box_widths, spectra)


def solution(mesh):
    in_specs = (P(("beam", "chan"), "tm"), P(), P())
    out_specs = P(("beam", "chan"), "tm")
    return jax.shard_map(local, mesh=mesh, in_specs=in_specs, out_specs=out_specs, check_vma=False)
```

```python
import functools

import jax
import jax.numpy as jnp
from jax import lax
from jax.experimental import pallas as pl
from jax.experimental.pallas import tpu as pltpu
from jax.sharding import PartitionSpec as P

SWAPS = 3
LANES = 128
SUB = 8
CHUNKS = 16
LAGS = (2, 4, 8)
MESH = pl.DeviceIdType.MESH


def kernel(shifts_ref, widths_ref, x_ref, out_ref, raw, y, recv, prev, amounts, done, edge, sums,
           load_sem, tail_send, tail_recv, send_sem, recv_sem, hist_send, hist_recv, out_sem):
    rows, time_len = x_ref.shape
    groups = rows // SUB
    levels = rows.bit_length() - 1
    sections = shifts_ref.shape[0]
    boxes = widths_ref.shape[0]
    hist = sections
    tiles = time_len // LANES
    per = tiles // CHUNKS
    chan, tm = lax.axis_index("chan"), lax.axis_index("tm")
    chans, tms = lax.axis_size("chan"), lax.axis_size("tm")
    chan_bits = chans.bit_length() - 1
    bits = [(chan // 2 ** (chan_bits - SWAPS + s)) % 2 for s in range(SWAPS)]
    peers = [chan + (1 - 2 * bits[s]) * 2 ** (chan_bits - SWAPS + s) for s in range(SWAPS)]

    def cols(first, count=1):
        return pl.ds(pl.multiple_of(first * LANES, LANES), count * LANES)

    load = pltpu.make_async_copy(x_ref, raw.at[:, pl.ds(hist * LANES, time_len)], load_sem)
    load.start()

    barrier = pltpu.get_barrier_semaphore()
    for s in range(SWAPS):
        pl.semaphore_signal(barrier, inc=1, device_id={"chan": peers[s]}, device_id_type=MESH)

    @pl.when(tm > 0)
    def _():
        pl.semaphore_signal(barrier, inc=1, device_id={"tm": tm - 1}, device_id_type=MESH)

    sub = lax.broadcasted_iota(jnp.int32, (SUB, LANES), 0)
    lane = lax.broadcasted_iota(jnp.int32, (SUB, LANES), 1)

    def fill(j, _):
        for g in range(groups):
            v = jnp.zeros((SUB, LANES), jnp.int32)
            for r in range(SUB):
                v = jnp.where(sub == r, shifts_ref[j, chan * rows + g * SUB + r], v)
            amounts[j, g * SUB:(g + 1) * SUB, :] = v
        return 0

    lax.fori_loop(0, sections, fill, 0)
    prev[...] = jnp.zeros_like(prev)

    pl.semaphore_wait(barrier, SWAPS + jnp.where(tm < tms - 1, 1, 0))

    def tail():
        return pltpu.make_async_remote_copy(
            src_ref=x_ref.at[:, pl.ds(time_len - hist * LANES, hist * LANES)],
            dst_ref=raw.at[:, pl.ds(0, hist * LANES)],
            send_sem=tail_send, recv_sem=tail_recv,
            device_id={"tm": (tm + 1) % tms}, device_id_type=MESH)

    @pl.when(tm < tms - 1)
    def _():
        tail().start()

    def swap(s, c):
        where = pl.ds(hist + c * per, per)
        return pltpu.make_async_remote_copy(
            src_ref=y.at[s, where], dst_ref=recv.at[s, where],
            send_sem=send_sem.at[s, c], recv_sem=recv_sem.at[s, c],
            device_id={"chan": peers[s]}, device_id_type=MESH)

    def swap_hist(s):
        first = levels - 1 + s
        where = pl.ds(first, hist - first)
        return pltpu.make_async_remote_copy(
            src_ref=y.at[s, where], dst_ref=recv.at[s, where],
            send_sem=hist_send.at[s], recv_sem=hist_recv.at[s],
            device_id={"chan": peers[s]}, device_id_type=MESH)

    def delayed(j, g, now, before):
        amount = amounts[j, g * SUB:(g + 1) * SUB, :]
        mixed = jnp.where(lane < LANES - amount, now, before)
        return jnp.take_along_axis(mixed, (lane - amount) & (LANES - 1), axis=1, mode="promise_in_bounds")

    def own_sections(first, count):
        kept = [[prev[j, g * SUB:(g + 1) * SUB, :] for g in range(groups)] for j in range(levels)]
        for t in range(count):
            k = first + t
            v = [raw[g * SUB:(g + 1) * SUB, cols(k)] for g in range(groups)]
            for j in range(levels):
                stride = 2 ** j
                if stride < SUB:
                    high = (sub & stride) != 0
                    low = [jnp.where(high, pltpu.roll(a, stride, 0), a) for a in v]
                    up = [jnp.where(high, a, pltpu.roll(a, SUB - stride, 0)) for a in v]
                else:
                    step = stride // SUB
                    low = [v[g & ~step] for g in range(groups)]
                    up = [v[g | step] for g in range(groups)]
                v = [low[g] + delayed(j, g, up[g], kept[j][g]) for g in range(groups)]
                kept[j] = up
            for g in range(groups):
                y[0, k, g * SUB:(g + 1) * SUB, :] = v[g]
        for j in range(levels):
            for g in range(groups):
                prev[j, g * SUB:(g + 1) * SUB, :] = kept[j][g]

    def swap_section(s, first, count, put):
        is_low = bits[s] == 0
        held = []
        for g in range(groups):
            rs = slice(g * SUB, (g + 1) * SUB)
            before = jnp.where(is_low, recv[s, first - 1, rs, :], y[s, first - 1, rs, :])
            own = [y[s, first + t, rs, :] for t in range(count)]
            other = [recv[s, first + t, rs, :] for t in range(count)]
            low = [jnp.where(is_low, a, b) for a, b in zip(own, other)]
            up = [jnp.where(is_low, b, a) for a, b in zip(own, other)]
            held.append((low, [before] + up))
        values = [[low[t] + delayed(levels + s, g, up[t + 1], up[t]) for t in range(count)]
                  for g, (low, up) in enumerate(held)]
        for g in range(groups):
            for t in range(count):
                put(g, t, values[g][t])

    def put_next(s, first):
        def put(g, t, value):
            y[s + 1, first + t, g * SUB:(g + 1) * SUB, :] = value
        return put

    def put_done(g, t, value):
        done[t * rows + g * SUB:t * rows + (g + 1) * SUB, :] = value

    a = lax.broadcasted_iota(jnp.int32, (LANES, 2 * LANES), 0)
    b = lax.broadcasted_iota(jnp.int32, (LANES, 2 * LANES), 1)
    ones = jnp.where(b < LANES, jnp.where(a <= b, 1.0, 0.0), jnp.where(a > b - LANES, -1.0, 0.0)).astype(jnp.bfloat16)

    def prefixes(x):
        total = None
        for _ in range(3):
            piece = x.astype(jnp.bfloat16)
            part = jnp.dot(piece, ones, preferred_element_type=jnp.float32)
            total = part if total is None else total + part
            x = x - piece.astype(jnp.float32)
        return total

    edge[...] = jnp.zeros_like(edge)

    @pl.when(tm == 0)
    def _():
        for s in range(SWAPS):
            y[s, hist - 1] = jnp.zeros((rows, LANES), jnp.float32)
            recv[s, hist - 1] = jnp.zeros((rows, LANES), jnp.float32)

    load.wait()

    @pl.when(tm > 0)
    def _():
        tail().wait_recv()
        own_sections(0, hist)
        swap_hist(0).start()

    box_lane = lax.broadcasted_iota(jnp.int32, (rows, LANES), 1)
    scale = 0.5 ** sections / boxes

    def out_copy(c):
        where = cols(c * per, per)
        return pltpu.make_async_copy(raw.at[:, where], out_ref.at[:, where], out_sem.at[c])

    def boxcars(c):
        sums[...] = prefixes(done[...])
        for t in range(per):
            now = sums[t * rows:(t + 1) * rows, :LANES]
            before = edge[...] if t == 0 else sums[(t - 1) * rows:t * rows, LANES:]
            power = jnp.zeros((rows, LANES), jnp.float32)
            for f in range(boxes):
                width = widths_ref[f]
                mixed = jnp.where(box_lane < LANES - width, now, before)
                window = now - pltpu.roll(mixed, width & (LANES - 1), 1)
                power = power + window * window * (scale / jnp.full((rows, LANES), width, jnp.int32).astype(jnp.float32))
            raw[:, cols(c * per + t)] = power
        edge[...] = sums[(per - 1) * rows:, LANES:]

    def step(i, _):
        @pl.when(i < CHUNKS)
        def _():
            own_sections(hist + i * per, per)
            swap(0, i).start()

        @pl.when((i >= LAGS[0]) & (i < CHUNKS + LAGS[0]))
        def _():
            c = i - LAGS[0]
            @pl.when((c == 0) & (tm > 0))
            def _():
                swap_hist(0).wait_recv()
                swap_section(0, levels, hist - levels, put_next(0, levels))
                swap_hist(1).start()
            swap(0, c).wait_recv()
            first = hist + c * per
            swap_section(0, first, per, put_next(0, first))
            swap(1, c).start()

        @pl.when((i >= LAGS[1]) & (i < CHUNKS + LAGS[1]))
        def _():
            c = i - LAGS[1]
            @pl.when((c == 0) & (tm > 0))
            def _():
                swap_hist(1).wait_recv()
                swap_section(1, levels + 1, hist - levels - 1, put_next(1, levels + 1))
                swap_hist(2).start()
            swap(1, c).wait_recv()
            first = hist + c * per
            swap_section(1, first, per, put_next(1, first))
            swap(2, c).start()

        @pl.when(i >= LAGS[2])
        def _():
            c = i - LAGS[2]
            @pl.when((c == 0) & (tm > 0))
            def _():
                swap_hist(2).wait_recv()
                swap_section(2, hist - 1, 1, put_done)
                edge[...] = prefixes(done[0:rows, :])[:, LANES:]
            swap(2, c).wait_recv()
            swap_section(2, hist + c * per, per, put_done)
            boxcars(c)
            out_copy(c).start()

        return 0

    lax.fori_loop(0, CHUNKS + LAGS[2], step, 0)

    def finish(c, _):
        for s in range(SWAPS):
            swap(s, c).wait_send()
        out_copy(c).wait()
        return 0

    lax.fori_loop(0, CHUNKS, finish, 0)

    @pl.when(tm > 0)
    def _():
        for s in range(SWAPS):
            swap_hist(s).wait_send()

    @pl.when(tm < tms - 1)
    def _():
        tail().wait_send()


def local(spectra, delay_shifts, box_widths):
    rows, time_len = spectra.shape
    sections = delay_shifts.shape[0]
    levels = rows.bit_length() - 1
    width = time_len + sections * LANES
    per = time_len // LANES // CHUNKS
    dma = pltpu.SemaphoreType.DMA
    return pl.pallas_call(
        kernel,
        out_shape=jax.ShapeDtypeStruct((rows, time_len), jnp.float32),
        in_specs=[pl.BlockSpec(memory_space=pltpu.SMEM), pl.BlockSpec(memory_space=pltpu.SMEM),
                  pl.BlockSpec(memory_space=pl.ANY)],
        out_specs=pl.BlockSpec(memory_space=pl.ANY),
        scratch_shapes=[
            pltpu.VMEM((rows, width), jnp.float32),
            pltpu.VMEM((SWAPS, width // LANES, rows, LANES), jnp.float32),
            pltpu.VMEM((SWAPS, width // LANES, rows, LANES), jnp.float32),
            pltpu.VMEM((levels, rows, LANES), jnp.float32),
            pltpu.VMEM((sections, rows, LANES), jnp.int32),
            pltpu.VMEM((per * rows, LANES), jnp.float32),
            pltpu.VMEM((rows, LANES), jnp.float32),
            pltpu.VMEM((per * rows, 2 * LANES), jnp.float32),
            dma(()), dma(()), dma(()),
            dma((SWAPS, CHUNKS)), dma((SWAPS, CHUNKS)),
            dma((SWAPS,)), dma((SWAPS,)), dma((CHUNKS,)),
        ],
        compiler_params=pltpu.CompilerParams(
            collective_id=0, has_side_effects=True, vmem_limit_bytes=60 * 1024 * 1024),
    )(delay_shifts, box_widths, spectra)


def solution(mesh):
    in_specs = (P(("beam", "chan"), "tm"), P(), P())
    out_specs = P(("beam", "chan"), "tm")
    return jax.shard_map(local, mesh=mesh, in_specs=in_specs, out_specs=out_specs, check_vma=False)
```
